256 devices in a mesh: dp: 32 (over y_hi, z, core), tensor: 8 (over y_lo, x).
Axes of the slice: x: 4, y: 4 (y_hi: 2, y_lo: 2; y = y_hi * 2 + y_lo), z: 8, core: 2. Of those that a mesh axis runs over, the one named last changes fastest.
Arguments:
- hidden_in: bfloat16 [32, 1024, 3072], P('dp', 'tensor'), may hold values from -6 to 6
- grad_out: bfloat16 [32, 1024, 3072], P('dp', 'tensor'), may hold values from -6 to 6
- saved_qkv: bfloat16 [32, 1024, 3, 2048], P('dp', None, None, 'tensor'), may hold values from -5.5 to 5.5
- saved_attn: bfloat16 [32, 1024, 2048], P('dp', None, 'tensor'), may hold values from -6 to 6
- w_qkv: bfloat16 [3072, 3, 2048], P(None, None, 'tensor'), may hold values from -0.109375 to 0.109375
- w_out: bfloat16 [3072, 2048], P(None, 'tensor'), may hold values from -0.125 to 0.125
- mod_table: bfloat16 [32, 2, 3, 3072], replicated, may hold values from -3 to 3
- timestep: int32 [32], P('dp'), may hold values from 0 to 31
- text_count: int32 [32], P('dp'), may hold values from 1 to 256
Outputs:
- grad_in: bfloat16 [32, 1024, 3072], P('dp', 'tensor')
- grad_w_qkv: float32 [3072, 3, 2048], P('dp', None, 'tensor')
- grad_w_out: float32 [3072, 2048], P('dp', 'tensor')
- grad_table: float32 [32, 2, 3, 3072], P('dp', None, None, 'tensor')
The draws below stay inside these ranges and needn't reach their ends.
All inputs are finite; a program needn't handle non-finite values.
Results may differ from the reference program's by a relative error of at most 0.02.
Values may be sent and summed in bfloat16 or wider, within the bound.
No kernel may reach another device: no remote copies, remote signals or barrier semaphores. Data moves between devices by JAX's collectives and lax.ppermute only.
A program may use at most 128 MiB of HBM per device.

```python
import jax
import jax.numpy as jnp
from jax import lax

D = 3072
HEAD_DIM = 128
HEADS = 16
TSTEPS = 32
SAMPLES = 32
SEQ = 1024
TXT = 256
HW = 2048
N_TENSOR = 8


def draw_saved_qkv(key, part):
    key = jax.random.fold_in(key, 11)
    base_key = jax.random.fold_in(key, 0)
    shape = (SAMPLES, SEQ, 3, HW)
    base = jnp.clip(jax.random.normal(base_key, shape, jnp.float32), -5.5, 5.5)
    return base.astype(jnp.bfloat16)


def draw_text_count(key, part):
    key = jax.random.fold_in(key, 23)
    count_key, which_key = jax.random.split(key)
    counts = jax.random.randint(count_key, (SAMPLES,), 1, TXT + 1)
    which = jax.random.randint(which_key, (), 0, SAMPLES)
    return counts.at[which].set(TXT).astype(jnp.int32)


def touch_ends(drawn, key, low, largest):
    extent = drawn.shape
    index_at = [jax.random.randint(jax.random.fold_in(key, axis), (), 0, extent[axis]) for axis in range(len(extent))]
    drawn = drawn.at[tuple(index_at)].set(low)
    longest = extent.index(max(extent))
    index_at[longest] = (index_at[longest] + 1) % extent[longest]
    return drawn.at[tuple(index_at)].set(largest)


def steps_of(rng, shape, cuts, smallest, largest):
    gain = 1.0
    for position, parts in cuts:
        draws = jax.random.uniform(jax.random.fold_in(jax.random.fold_in(rng, 6), position), (parts,), jnp.float32, smallest / len(cuts), largest / len(cuts))
        gain = gain * jnp.repeat(jnp.exp(draws), shape[position] // parts).reshape((-1,) + (1,) * (len(shape) - 1 - position))
    return gain


def centred(rng, dims, deviation, reach, shards=(), held_as=jnp.bfloat16):
    values = deviation * jax.random.normal(rng, dims, jnp.float32)
    if shards:
        values = values * steps_of(rng, dims, shards, -0.22, 0.18)
    return jnp.clip(values, -reach, reach).astype(held_as)


def setup_inputs(seed: int = 0) -> dict:
    arg_keys = jax.random.split(jax.random.key(seed), 10)
    hidden_in = centred(arg_keys[0], (SAMPLES, SEQ, D), 1.0, 6.0, ((0, 32), (1, 8)))
    grad_out = centred(arg_keys[1], (SAMPLES, SEQ, D), 1.0, 6.0, ((0, 32), (1, 8)))
    saved_qkv = draw_saved_qkv(jax.random.fold_in(arg_keys[9], 71), 0)
    saved_attn = centred(arg_keys[3], (SAMPLES, SEQ, HW), 1.0, 6.0, ((0, 32), (2, 8)))
    w_qkv = centred(arg_keys[4], (D, 3, HW), D ** -0.5, 0.109375, ((2, 8),))
    w_out = centred(arg_keys[5], (D, HW), HW ** -0.5, 0.125, ((1, 8),))
    mod_table = centred(arg_keys[6], (TSTEPS, 2, 3, D), 0.5, 3.0)
    timestep = touch_ends(jax.random.randint(arg_keys[7], (SAMPLES,), 0, TSTEPS), jax.random.fold_in(arg_keys[7], 1), 0, TSTEPS - 1).astype(jnp.int32)
    text_count = draw_text_count(jax.random.fold_in(arg_keys[9], 71), 0)
    return {"hidden_in": hidden_in, "grad_out": grad_out, "saved_qkv": saved_qkv, "saved_attn": saved_attn, "w_qkv": w_qkv, "w_out": w_out, "mod_table": mod_table, "timestep": timestep, "text_count": text_count}


norm_eps = 1e-06
masked_score = -1e+30

def stream_pick(modulation, positions, which):
    image_rows = (positions >= TXT)[:, None]
    return jnp.where(image_rows, modulation[1, which], modulation[0, which])

def head_backward(operands, key_valid):
    query, key_mat, value_mat, attn_head = operands
    score_scale = HEAD_DIM ** (-0.5)
    scores = jnp.dot(query, key_mat.T, preferred_element_type=jnp.float32) * score_scale
    scores = jnp.where(key_valid[None, :], scores, masked_score)
    row_max = lax.optimization_barrier(jnp.max(scores, axis=1, keepdims=True))
    exp_scores = jnp.exp(scores - row_max)
    attn_probs = exp_scores / lax.optimization_barrier(jnp.sum(exp_scores, axis=1, keepdims=True))
    value_grad = jnp.dot(attn_probs.astype(jnp.bfloat16).T, attn_head, preferred_element_type=jnp.float32)
    prob_grad = jnp.dot(attn_head, value_mat.T, preferred_element_type=jnp.float32)
    delta_rows = lax.optimization_barrier(jnp.sum(attn_probs * prob_grad, axis=1, keepdims=True))
    score_grad = (attn_probs * (prob_grad - delta_rows) * score_scale).astype(jnp.bfloat16)
    query_grad = jnp.dot(score_grad, key_mat, preferred_element_type=jnp.float32)
    key_grad = jnp.dot(score_grad.T, query, preferred_element_type=jnp.float32)
    return (query_grad.astype(jnp.bfloat16), key_grad.astype(jnp.bfloat16), value_grad.astype(jnp.bfloat16))

def split_heads(matrix):
    return matrix.reshape(SEQ, HEADS, HEAD_DIM).transpose(1, 0, 2)

def join_heads(matrix):
    return matrix.transpose(1, 0, 2).reshape(SEQ, HW)

def reference(hidden_in, grad_out, saved_qkv, saved_attn, w_qkv, w_out, mod_table, timestep, text_count):
    table_f = mod_table.astype(jnp.float32)
    wout_f = w_out.astype(jnp.float32)
    group_width = HW // N_TENSOR

    def sample_backward(totals, sample):
        acc_qkv, acc_out, acc_table = totals
        hidden, grad, qkv_saved, attn_saved, step_index, text_len = sample
        selector = (jnp.arange(TSTEPS, dtype=jnp.int32) == step_index).astype(jnp.float32)
        modulation = jnp.einsum('t,tscd->scd', selector, table_f)
        positions = jnp.arange(SEQ, dtype=jnp.int32)
        shift_rows = stream_pick(modulation, positions, 0)
        scale_rows = stream_pick(modulation, positions, 1)
        gate_rows = stream_pick(modulation, positions, 2)
        hidden_f = hidden.astype(jnp.float32)
        centered = hidden_f - lax.optimization_barrier(jnp.mean(hidden_f, axis=1, keepdims=True))
        inv_std = lax.rsqrt(lax.optimization_barrier(jnp.mean(centered * centered, axis=1, keepdims=True)) + norm_eps)
        normed = centered * inv_std
        mixed_in = (normed * (1.0 + scale_rows) + shift_rows).astype(jnp.bfloat16)
        out_grad = (gate_rows * grad.astype(jnp.float32)).astype(jnp.bfloat16)
        attn_grad = jnp.dot(out_grad, w_out, preferred_element_type=jnp.float32).astype(jnp.bfloat16)
        text_prod = jnp.dot(grad[:TXT].T, attn_saved[:TXT], preferred_element_type=jnp.float32)
        image_prod = jnp.dot(grad[TXT:].T, attn_saved[TXT:], preferred_element_type=jnp.float32)
        out_weight = modulation[0, 2][:, None] * text_prod + modulation[1, 2][:, None] * image_prod
        gate_text = lax.optimization_barrier(jnp.sum(wout_f * text_prod, axis=1))
        gate_image = lax.optimization_barrier(jnp.sum(wout_f * image_prod, axis=1))
        key_valid = (positions >= TXT) | (positions < text_len)
        operands = (split_heads(qkv_saved[:, 0]), split_heads(qkv_saved[:, 1]), split_heads(qkv_saved[:, 2]), split_heads(attn_grad))
        head_grads = lax.map(lambda ops: head_backward(ops, key_valid), operands)
        grad_qkv = jnp.stack([join_heads(part_grad) for part_grad in head_grads], axis=1)

        def add_group(mixed_total, group_index):
            begin_col = (group_index * group_width).astype(jnp.int32)
            qkv_cols = lax.dynamic_slice_in_dim(grad_qkv, begin_col, group_width, 2)
            weight_cols = lax.dynamic_slice_in_dim(w_qkv, begin_col, group_width, 2)
            group_term = jnp.einsum('scj,dcj->sd', qkv_cols.astype(jnp.float32), weight_cols.astype(jnp.float32))
            rounded = lax.optimization_barrier(group_term.astype(jnp.bfloat16))
            return (mixed_total + rounded.astype(jnp.float32), None)
        mixed_grad, unused = lax.scan(add_group, jnp.zeros((SEQ, D), jnp.float32), jnp.arange(N_TENSOR, dtype=jnp.int32))
        qkv_weight = jnp.einsum('sd,scj->dcj', mixed_in.astype(jnp.float32), grad_qkv.astype(jnp.float32))
        image_rows = (positions >= TXT)[:, None]
        shift_text = lax.optimization_barrier(jnp.sum(jnp.where(image_rows, 0.0, mixed_grad), axis=0))
        shift_image = lax.optimization_barrier(jnp.sum(jnp.where(image_rows, mixed_grad, 0.0), axis=0))
        scale_text = lax.optimization_barrier(jnp.sum(jnp.where(image_rows, 0.0, mixed_grad * normed), axis=0))
        scale_image = lax.optimization_barrier(jnp.sum(jnp.where(image_rows, mixed_grad * normed, 0.0), axis=0))
        scaled = mixed_grad * (1.0 + scale_rows)
        branch = inv_std * (scaled - lax.optimization_barrier(jnp.mean(scaled, axis=1, keepdims=True)) - normed * lax.optimization_barrier(jnp.mean(scaled * normed, axis=1, keepdims=True)))
        mod_grad = jnp.stack([jnp.stack([shift_text, scale_text, gate_text]), jnp.stack([shift_image, scale_image, gate_image])])
        totals = (acc_qkv + qkv_weight, acc_out + out_weight, acc_table + selector[:, None, None, None] * mod_grad)
        return (totals, branch.astype(jnp.bfloat16))
    start_totals = (jnp.zeros((D, 3, HW), jnp.float32), jnp.zeros((D, HW), jnp.float32), jnp.zeros((TSTEPS, 2, 3, D), jnp.float32))
    totals, grad_in = lax.scan(sample_backward, start_totals, (hidden_in, grad_out, saved_qkv, saved_attn, timestep, text_count))
    return (grad_in, totals[0], totals[1], totals[2])
```

```python
import math

import jax
import jax.numpy as jnp
from jax import lax
from jax.sharding import Mesh
from jax.sharding import PartitionSpec as P

HEAD_DIM = 128
AXES = {"yh": 2, "z": 8, "c": 2, "yl": 2, "x": 4}
Y = ("yh", "yl")

norm_eps = 1e-06
masked_score = -1e30
bf16 = jnp.bfloat16
f32 = jnp.float32


def ring(array, axis, step):
    size = AXES[axis] if isinstance(axis, str) else math.prod(AXES[name] for name in axis)
    return lax.ppermute(array, axis, [(i, (i + step) % size) for i in range(size)])


def swap_core(array):
    return lax.ppermute(array, "c", [(0, 1), (1, 0)])


def rehome(array):
    return lax.ppermute(array, ("c", "yl"), [(0, 0), (1, 2), (2, 1), (3, 3)])


def weight_route(own_pair):
    route = []
    for yh in range(2):
        for c in range(2):
            for yl in range(2):
                dest = yh * 4 + c * 2 + yl
                if c == yl:
                    route.append((dest, dest))
                    continue
                chip = yh * 2 + yl
                source = (chip ^ 1) if own_pair else (3 - chip)
                route.append(((source // 2) * 4 + (1 - source % 2) * 2 + source % 2, dest))
    return route


def move_weight(array, own_pair):
    return lax.ppermute(array, ("yh", "c", "yl"), weight_route(own_pair))


def pick(array, index):
    return lax.dynamic_index_in_dim(array, index, 0, False)


def rows_product(left, right):
    return lax.dot_general(left, right, (((0,), (0,)), ((), ())), preferred_element_type=f32)


def gather_rows(own, c, x):
    rows = own.shape[0]
    whole = jnp.zeros((8 * rows, own.shape[1]), own.dtype)
    for step in range(4):
        part = own if step == 0 else ring(own, "x", step)
        other = swap_core(part)
        place = (x + 4 - step) % 4
        whole = lax.dynamic_update_slice(whole, part, ((c * 4 + place) * rows, 0))
        whole = lax.dynamic_update_slice(whole, other, (((1 - c) * 4 + place) * rows, 0))
    return whole


def attention_grads(queries, keys, values, attn_grad, text_count, text_len):
    seq_len = queries.shape[0]
    heads = queries.shape[1] // HEAD_DIM
    all_pos = jnp.arange(seq_len, dtype=jnp.int32)
    key_valid = (all_pos >= text_len) | (all_pos < text_count)
    score_scale = HEAD_DIM ** (-0.5)
    grads = ([], [], [])
    for head in range(heads):
        cols = slice(head * HEAD_DIM, (head + 1) * HEAD_DIM)
        q, k, v, g = queries[:, cols], keys[:, cols], values[:, cols], attn_grad[:, cols]
        scores = jnp.dot(k, q.T, preferred_element_type=f32) * score_scale
        scores = jnp.where(key_valid[:, None], scores, masked_score)
        exp_scores = jnp.exp(scores - jnp.max(scores, axis=0, keepdims=True))
        probs = exp_scores / jnp.sum(exp_scores, axis=0, keepdims=True)
        prob_grad = jnp.dot(v, g.T, preferred_element_type=f32)
        delta = jnp.sum(probs * prob_grad, axis=0, keepdims=True)
        score_grad = (probs * (prob_grad - delta) * score_scale).astype(bf16)
        grads[0].append(rows_product(score_grad, k).astype(bf16))
        grads[1].append(jnp.dot(score_grad, q, preferred_element_type=f32).astype(bf16))
        grads[2].append(jnp.dot(probs.astype(bf16), g, preferred_element_type=f32).astype(bf16))
    return jnp.stack([jnp.concatenate(grad, axis=1) for grad in grads])


def reduce_samples(term, yh_yl, z):
    count = term.shape[0]
    chunks = term.reshape(count, 2, 8, 2, 96, 256).transpose(1, 3, 0, 2, 4, 5)
    chunks = chunks.reshape(4, count, 8, 96, 256)
    total = pick(chunks, yh_yl).astype(f32)
    for step in range(1, 4):
        total += ring(pick(chunks, (yh_yl + step) % 4), Y, step).astype(f32)
    chunks = total.astype(bf16).transpose(1, 0, 2, 3)
    total = pick(chunks, z).astype(f32)
    for step in range(1, 8):
        total += ring(pick(chunks, (z + step) % 8), "z", step).astype(f32)
    return total


def per_device(
    hidden_in, grad_out, saved_qkv, saved_attn, w_qkv, w_out, mod_table, timestep, text_count
):
    c, yl, x = (lax.axis_index(name) for name in ("c", "yl", "x"))
    yh, z = lax.axis_index("yh"), lax.axis_index("z")
    chip_y = yh * 2 + yl
    shard_rows, width = hidden_in.shape[1:]
    seq_len = saved_qkv.shape[1]
    text_len = seq_len // 4
    first_row = (c * 4 + x) * shard_rows

    grad_own = rehome(grad_out[0])
    numbers = rehome(jnp.concatenate([timestep, text_count]))
    hidden_own = rehome(hidden_in[0])
    qkv = rehome(saved_qkv[0].transpose(1, 0, 2))
    attn = rehome(saved_attn[0])
    weights = w_qkv.transpose(1, 0, 2)
    wout = move_weight(w_out, False)
    w_kv = move_weight(weights[1:], False)
    w_q = move_weight(weights[0], True)

    selector = (jnp.arange(mod_table.shape[0], dtype=jnp.int32) == numbers[0]).astype(f32)
    modulation = jnp.einsum("t,tscd->scd", selector, mod_table.astype(f32))

    grad_all = gather_rows(grad_own, c, x)
    hidden_f = hidden_own.astype(f32)
    centered = hidden_f - jnp.mean(hidden_f, axis=1, keepdims=True)
    inv_std = lax.rsqrt(jnp.mean(centered * centered, axis=1, keepdims=True) + norm_eps)
    normed = centered * inv_std
    normed_all = gather_rows(normed.astype(bf16), c, x)

    image_all = (jnp.arange(seq_len, dtype=jnp.int32) >= text_len)[:, None]
    gate_rows = jnp.where(image_all, modulation[1, 2], modulation[0, 2])
    out_grad = (gate_rows * grad_all.astype(f32)).astype(bf16)
    attn_grad = jnp.dot(out_grad, wout, preferred_element_type=f32).astype(bf16)

    text_prod = rows_product(grad_all[:text_len], attn[:text_len])
    image_prod = rows_product(grad_all[text_len:], attn[text_len:])
    out_term = modulation[0, 2][:, None] * text_prod + modulation[1, 2][:, None] * image_prod
    wout_f = wout.astype(f32)
    gate_text = jnp.sum(wout_f * text_prod, axis=1)
    gate_image = jnp.sum(wout_f * image_prod, axis=1)
    grad_w_out = reduce_samples(out_term.astype(bf16)[None], chip_y, z)[0]

    grad_qkv = attention_grads(qkv[0], qkv[1], qkv[2], attn_grad, numbers[1], text_len)

    w_parts = (w_q, w_kv[0], w_kv[1])
    partial = sum(
        lax.dot_general(
            grad_qkv[i], w_parts[i], (((1,), (1,)), ((), ())), preferred_element_type=f32
        )
        for i in range(3)
    ).astype(bf16)
    partial = partial.reshape(2, 4, shard_rows, width)
    got = swap_core(pick(partial, 1 - c))
    half = (pick(partial, c).astype(f32) + got.astype(f32)).astype(bf16)
    mixed_grad = pick(half, x).astype(f32)
    for step in range(1, 4):
        mixed_grad += ring(pick(half, (x + step) % 4), "x", step).astype(f32)

    terms, scale_grads, shift_grads = [], [[], []], [[], []]
    for i in range(3):
        weight_f = w_parts[i].astype(f32)
        term = 0.0
        for stream, rows in enumerate((slice(0, text_len), slice(text_len, seq_len))):
            prod = rows_product(normed_all[rows], grad_qkv[i][rows])
            col_sum = jnp.sum(grad_qkv[i][rows].astype(f32), axis=0)
            term += (1.0 + modulation[stream, 1][:, None]) * prod
            term += modulation[stream, 0][:, None] * col_sum
            scale_grads[stream].append(jnp.sum(weight_f * prod, axis=1))
            shift_grads[stream].append(jnp.sum(weight_f * col_sum, axis=1))
        terms.append(term.astype(bf16))
    grad_w_qkv = reduce_samples(jnp.stack(terms), chip_y, z)

    mod_grad = jnp.stack(
        [
            sum(shift_grads[0]), sum(scale_grads[0]), gate_text,
            sum(shift_grads[1]), sum(scale_grads[1]), gate_image,
        ]
    )
    pieces = mod_grad.reshape(6, 2, 4, width // 8).transpose(1, 2, 0, 3)
    pieces = pick(pieces, c) + swap_core(pick(pieces, 1 - c))
    own_mod = pick(pieces, x)
    for step in range(1, 4):
        own_mod += ring(pick(pieces, (x + step) % 4), "x", step)
    stamp = jnp.full((2, width // 8), numbers[0].astype(f32))
    stamped = jnp.concatenate([own_mod, stamp])[None]
    stamped = jnp.concatenate([stamped] + [ring(stamped, "z", step) for step in range(1, 8)])
    stamped = jnp.concatenate([stamped] + [ring(stamped, Y, step) for step in range(1, 4)])
    table_row = (yh * 16 + z * 2 + yl).astype(f32)
    table = jnp.sum(jnp.where(stamped[:, 6:7] == table_row, stamped[:, :6], 0.0), axis=0)
    grad_table = rehome(table).reshape(1, 2, 3, width // 8)

    image_own = first_row >= text_len
    scale_own = jnp.where(image_own, modulation[1, 1], modulation[0, 1])[None]
    scaled = mixed_grad * (1.0 + scale_own)
    branch = inv_std * (
        scaled
        - jnp.mean(scaled, axis=1, keepdims=True)
        - normed * jnp.mean(scaled * normed, axis=1, keepdims=True)
    )
    grad_in = rehome(branch.astype(bf16))[None]
    grad_w = rehome(jnp.concatenate([grad_w_qkv, grad_w_out[None]]).astype(bf16)).astype(f32)
    return (grad_in, grad_w[:3].transpose(1, 0, 2), grad_w[3], grad_table)


def solution(mesh):
    fine = Mesh(mesh.devices.reshape(tuple(AXES.values())), tuple(AXES))
    dp, tensor = ("yh", "z", "c"), ("yl", "x")
    in_specs = (
        P(dp, tensor, None),
        P(dp, tensor, None),
        P(dp, None, None, tensor),
        P(dp, None, tensor),
        P(None, None, tensor),
        P(None, tensor),
        P(),
        P(dp),
        P(dp),
    )
    out_specs = (
        P(dp, tensor, None),
        P(dp, None, tensor),
        P(dp, tensor),
        P(dp, None, None, tensor),
    )
    return jax.shard_map(
        per_device, mesh=fine, in_specs=in_specs, out_specs=out_specs, check_vma=False
    )
```

```python
import math

import jax
import jax.numpy as jnp
from jax import lax
from jax.experimental import pallas as pl
from jax.experimental.pallas import tpu as pltpu
from jax.sharding import Mesh
from jax.sharding import PartitionSpec as P

HEAD_DIM = 128
AXES = {"yh": 2, "z": 8, "c": 2, "yl": 2, "x": 4}
Y = ("yh", "yl")

norm_eps = 1e-06
masked_score = -1e30
bf16 = jnp.bfloat16
f32 = jnp.float32
D_TILE = 384
VMEM_LIMIT = 60 * 1024 * 1024


def ring(array, axis, step):
    size = AXES[axis] if isinstance(axis, str) else math.prod(AXES[name] for name in axis)
    return lax.ppermute(array, axis, [(i, (i + step) % size) for i in range(size)])


def swap_core(array):
    return lax.ppermute(array, "c", [(0, 1), (1, 0)])


def rehome(array):
    return jnp.where(stays(), array, lax.ppermute(array, ("c", "yl"), [(1, 2), (2, 1)]))


def stays():
    return lax.axis_index("c") == lax.axis_index("yl")


def move_weight(array):
    route = [(1, 6), (2, 5), (5, 2), (6, 1)]
    return lax.ppermute(array, ("yh", "c", "yl"), route)


def pick(array, index):
    return lax.dynamic_index_in_dim(array, index, 0, False)


def rows_product(left, right):
    return lax.dot_general(left, right, (((0,), (0,)), ((), ())), preferred_element_type=f32)


def cols_product(left, right):
    return lax.dot_general(left, right, (((1,), (1,)), ((), ())), preferred_element_type=f32)


def after(array, *earlier):
    return lax.optimization_barrier((array,) + earlier)[0]


def row_sums(array):
    folded = array[:, :128]
    for begin in range(128, array.shape[1], 128):
        folded += array[:, begin : begin + 128]
    return jnp.sum(folded.T, axis=0, keepdims=True)


def gather_pieces(own, x, c, *earlier):
    rows = own.shape[0]
    half = rows // 2
    left, right = ring(after(own, *earlier), "x", 1), ring(after(own, *earlier), "x", 3)
    far_left, far_right = ring(left[:half], "x", 1), ring(right[half:], "x", 3)
    mine = [own, left, right, far_left, far_right]
    places = [x * rows, (x + 3) % 4 * rows, (x + 1) % 4 * rows]
    places += [(x + 2) % 4 * rows, (x + 2) % 4 * rows + half]
    theirs = [swap_core(piece) for piece in mine]
    firsts = [c * 4 * rows + place for place in places]
    firsts += [(1 - c) * 4 * rows + place for place in places]
    scalars = [stays().astype(jnp.int32), jnp.int32(0)] + firsts
    return mine + theirs, jnp.stack(scalars).astype(jnp.int32)


def assemble(firsts_ref, piece_refs, whole):
    for index, piece in enumerate(piece_refs):
        first = pl.multiple_of(firsts_ref[2 + index], 64)
        whole[pl.ds(first, piece.shape[0]), :] = piece[...]


def choose(scalars_ref, own_ref, moved_ref, weight):
    @pl.when(scalars_ref[0] == 1)
    def _():
        weight[...] = own_ref[...]

    @pl.when(scalars_ref[0] != 1)
    def _():
        weight[...] = moved_ref[...]


def weight_specs(shape):
    lead = (0,) * (len(shape) - 2)
    return [
        pl.BlockSpec(shape, lambda i, scalars: lead + (i * scalars[0], 0)),
        pl.BlockSpec(shape, lambda i, scalars: lead + (i * (1 - scalars[0]), 0)),
    ]


def piece_specs(pieces):
    return [pl.BlockSpec((piece.shape[0], D_TILE), lambda i, *_: (0, i)) for piece in pieces]


def store_chunks(out_ref, values, column):
    for z in range(2):
        for yl in range(2):
            begin = (z * 2 + yl) * 96
            out_ref[0, yl, z, column] = values[begin : begin + 96].astype(out_ref.dtype)


def grad_kernel(text_len, firsts_ref, *refs):
    pieces, (gate_ref, cols_ref, own_ref, moved_ref, attn_ref) = refs[:10], refs[10:15]
    grad_ref, term_ref, gate_out_ref, whole, total, wout = refs[15:]
    step = pl.program_id(0)
    assemble(firsts_ref, pieces, whole)
    choose(firsts_ref, own_ref, moved_ref, wout)
    grads = whole[...]
    weight = wout[...]
    gate = gate_ref[...]
    scaled = [
        (grads[rows].astype(f32) * gate[stream : stream + 1]).astype(bf16)
        for stream, rows in ((0, slice(0, text_len)), (1, slice(text_len, None)))
    ]
    product = jnp.dot(jnp.concatenate(scaled), weight, preferred_element_type=f32)

    @pl.when(step == 0)
    def _():
        total[...] = product

    @pl.when(step > 0)
    def _():
        total[...] += product

    @pl.when(step == pl.num_programs(0) - 1)
    def _():
        grad_ref[...] = total[...].astype(bf16)

    attn = attn_ref[...]
    text = rows_product(grads[:text_len], attn[:text_len])
    image = rows_product(grads[text_len:], attn[text_len:])
    weight_f = weight.astype(f32)
    gate_out_ref[0:1] = row_sums(weight_f * text)
    gate_out_ref[1:2] = row_sums(weight_f * image)
    store_chunks(term_ref, cols_ref[:, 2:3] * text + cols_ref[:, 5:6] * image, 0)


def grad_products(pieces, firsts, gates, cols, wouts, attn, text_len):
    seq_len, (width, columns) = attn.shape[0], wouts[0].shape
    steps = width // D_TILE
    return pl.pallas_call(
        lambda *refs: grad_kernel(text_len, *refs),
        grid_spec=pltpu.PrefetchScalarGridSpec(
            num_scalar_prefetch=1,
            grid=(steps,),
            in_specs=piece_specs(pieces)
            + [
                pl.BlockSpec((8, D_TILE), lambda i, *_: (0, i)),
                pl.BlockSpec((D_TILE, 8), lambda i, *_: (i, 0)),
                *weight_specs((D_TILE, columns)),
                pl.BlockSpec((seq_len, columns), lambda i, *_: (0, 0)),
            ],
            out_specs=[
                pl.BlockSpec((seq_len, columns), lambda i, *_: (0, 0)),
                pl.BlockSpec(
                    (1, 2, 2, 1, 96, columns), lambda i, *_: (i // 4, 0, i % 4, 0, 0, 0)
                ),
                pl.BlockSpec((8, D_TILE), lambda i, *_: (0, i)),
            ],
            scratch_shapes=[
                pltpu.VMEM((seq_len, D_TILE), bf16),
                pltpu.VMEM((seq_len, columns), f32),
                pltpu.VMEM((D_TILE, columns), bf16),
            ],
        ),
        out_shape=[
            jax.ShapeDtypeStruct((seq_len, columns), bf16),
            jax.ShapeDtypeStruct((2, 2, 8, 1, 96, columns), bf16),
            jax.ShapeDtypeStruct((8, width), f32),
        ],
        compiler_params=pltpu.CompilerParams(vmem_limit_bytes=VMEM_LIMIT),
        cost_estimate=pl.CostEstimate(
            flops=4 * seq_len * width * columns, bytes_accessed=12 * 2**20, transcendentals=0
        ),
        name="grad_products",
    )(firsts, *pieces, gates, cols, *wouts, attn)


def attention_kernel(text_len, count_ref, q_ref, k_ref, v_ref, g_ref, dq_ref, dkv_ref, dk, dv):
    block = pl.program_id(1)
    q, k, v, g = q_ref[0], k_ref[0], v_ref[0], g_ref[...]
    scale = HEAD_DIM ** (-0.5)
    scores = cols_product(k, q)
    position = lax.broadcasted_iota(jnp.int32, (text_len, 1), 0)
    masked = jnp.where(position < count_ref[0], scores[:text_len], masked_score)
    scores = jnp.concatenate([masked, scores[text_len:]])
    exps = jnp.exp2((scores - jnp.max(scores, axis=0, keepdims=True)) * (scale * math.log2(math.e)))
    inverse = 1.0 / jnp.sum(exps, axis=0, keepdims=True)
    probs = exps * inverse
    prob_grad = cols_product(v, g)
    delta = jnp.sum(probs * prob_grad, axis=0, keepdims=True)
    score_grad = (probs * (prob_grad - delta)).astype(bf16)
    dq_ref[0] = (rows_product(score_grad, k) * scale).astype(bf16)
    key_part = jnp.dot(score_grad, q, preferred_element_type=f32)
    value_part = jnp.dot(probs.astype(bf16), g, preferred_element_type=f32)

    @pl.when(block == 0)
    def _():
        dk[...] = key_part
        dv[...] = value_part

    @pl.when(block > 0)
    def _():
        dk[...] += key_part
        dv[...] += value_part

    @pl.when(block == pl.num_programs(1) - 1)
    def _():
        dkv_ref[0] = (dk[...] * scale).astype(bf16)
        dkv_ref[1] = dv[...].astype(bf16)


def attention_grads(qkv, attn_grad, text_count, text_len):
    seq_len, columns = attn_grad.shape
    heads, rows = columns // HEAD_DIM, 256
    return pl.pallas_call(
        lambda *refs: attention_kernel(text_len, *refs),
        grid_spec=pltpu.PrefetchScalarGridSpec(
            num_scalar_prefetch=1,
            grid=(heads, seq_len // rows),
            in_specs=[
                pl.BlockSpec((1, rows, HEAD_DIM), lambda h, i, *_: (0, i, h)),
                pl.BlockSpec((1, seq_len, HEAD_DIM), lambda h, i, *_: (1, 0, h)),
                pl.BlockSpec((1, seq_len, HEAD_DIM), lambda h, i, *_: (2, 0, h)),
                pl.BlockSpec((rows, HEAD_DIM), lambda h, i, *_: (i, h)),
            ],
            out_specs=[
                pl.BlockSpec((1, rows, HEAD_DIM), lambda h, i, *_: (0, i, h)),
                pl.BlockSpec((2, seq_len, HEAD_DIM), lambda h, i, *_: (0, 0, h)),
            ],
            scratch_shapes=[
                pltpu.VMEM((seq_len, HEAD_DIM), f32),
                pltpu.VMEM((seq_len, HEAD_DIM), f32),
            ],
        ),
        out_shape=[
            jax.ShapeDtypeStruct((1, seq_len, columns), bf16),
            jax.ShapeDtypeStruct((2, seq_len, columns), bf16),
        ],
        compiler_params=pltpu.CompilerParams(vmem_limit_bytes=VMEM_LIMIT),
        cost_estimate=pl.CostEstimate(
            flops=10 * seq_len * seq_len * columns,
            bytes_accessed=4 * 2**20,
            transcendentals=heads * seq_len * seq_len,
        ),
        name="attention_grads",
    )(text_count, qkv, qkv, qkv, attn_grad)


def mixed_kernel(scalars_ref, q_ref, kv_ref, own_ref, moved_ref, out_ref, w_ref):
    choose(scalars_ref, own_ref, moved_ref, w_ref)
    total = cols_product(q_ref[0], w_ref[0])
    total += cols_product(kv_ref[0], w_ref[1])
    total += cols_product(kv_ref[1], w_ref[2])
    out_ref[...] = total.astype(bf16)


def mixed_half(scalars, grad_q, grad_kv, weights):
    seq_len, columns = grad_q.shape[1:]
    width, rows, tile = weights[0].shape[1], seq_len // 2, 512
    return pl.pallas_call(
        mixed_kernel,
        grid_spec=pltpu.PrefetchScalarGridSpec(
            num_scalar_prefetch=1,
            grid=(width // tile,),
            in_specs=[
                pl.BlockSpec((1, rows, columns), lambda i, scalars: (0, scalars[1], 0)),
                pl.BlockSpec((2, rows, columns), lambda i, scalars: (0, scalars[1], 0)),
                *weight_specs((3, tile, columns)),
            ],
            out_specs=pl.BlockSpec((rows, tile), lambda i, *_: (0, i)),
            scratch_shapes=[pltpu.VMEM((3, tile, columns), bf16)],
        ),
        out_shape=jax.ShapeDtypeStruct((rows, width), bf16),
        compiler_params=pltpu.CompilerParams(vmem_limit_bytes=VMEM_LIMIT),
        cost_estimate=pl.CostEstimate(
            flops=6 * rows * width * columns, bytes_accessed=8 * 2**20, transcendentals=0
        ),
        name="mixed_half",
    )(scalars, grad_q, grad_kv, *weights)


def weight_kernel(text_len, firsts_ref, *refs):
    pieces, (cols_ref, own_ref, moved_ref, gq_ref, gkv_ref) = refs[:10], refs[10:15]
    term_ref, sums_ref, whole, col_sums, w_ref = refs[15:]
    streams = (slice(0, text_len), slice(text_len, None))
    grads = [gq_ref[0], gkv_ref[0], gkv_ref[1]]

    @pl.when(pl.program_id(0) == 0)
    def _():
        for i in range(3):
            for stream, rows in enumerate(streams):
                col_sums[i, stream : stream + 1] = jnp.sum(
                    grads[i][rows].astype(f32), axis=0, keepdims=True
                )

    assemble(firsts_ref, pieces, whole)
    choose(firsts_ref, own_ref, moved_ref, w_ref)
    turned = whole[...].T
    cols = cols_ref[...]
    shift_sums = jnp.zeros((2, D_TILE), f32)
    scaled = [0.0, 0.0]
    for i in range(3):
        weight = w_ref[i]
        weight_f = weight.astype(f32)
        sums = col_sums[i, 0:2]
        high = sums.astype(bf16)
        low = (sums - high.astype(f32)).astype(bf16)
        shift_sums += cols_product(high, weight) + cols_product(low, weight)
        term = 0.0
        for stream, rows in enumerate(streams):
            prod = jnp.dot(turned[:, rows], grads[i][rows], preferred_element_type=f32)
            term += cols[:, 3 * stream + 1 : 3 * stream + 2] * prod
            term += cols[:, 3 * stream : 3 * stream + 1] * sums[stream : stream + 1]
            scaled[stream] += weight_f * prod
        store_chunks(term_ref, term, i)
    sums_ref[0:2] = shift_sums
    sums_ref[2:3] = row_sums(scaled[0])
    sums_ref[3:4] = row_sums(scaled[1])


def weight_products(pieces, firsts, cols, weights, grad_q, grad_kv, text_len):
    _, width, columns = weights[0].shape
    seq_len = grad_q.shape[1]
    return pl.pallas_call(
        lambda *refs: weight_kernel(text_len, *refs),
        grid_spec=pltpu.PrefetchScalarGridSpec(
            num_scalar_prefetch=1,
            grid=(width // D_TILE,),
            in_specs=piece_specs(pieces)
            + [
                pl.BlockSpec((D_TILE, 8), lambda i, *_: (i, 0)),
                *weight_specs((3, D_TILE, columns)),
                pl.BlockSpec((1, seq_len, columns), lambda i, *_: (0, 0, 0)),
                pl.BlockSpec((2, seq_len, columns), lambda i, *_: (0, 0, 0)),
            ],
            out_specs=[
                pl.BlockSpec(
                    (1, 2, 2, 3, 96, columns), lambda i, *_: (i // 4, 0, i % 4, 0, 0, 0)
                ),
                pl.BlockSpec((8, D_TILE), lambda i, *_: (0, i)),
            ],
            scratch_shapes=[
                pltpu.VMEM((seq_len, D_TILE), bf16),
                pltpu.VMEM((3, 8, columns), f32),
                pltpu.VMEM((3, D_TILE, columns), bf16),
            ],
        ),
        out_shape=[
            jax.ShapeDtypeStruct((2, 2, 8, 3, 96, columns), bf16),
            jax.ShapeDtypeStruct((8, width), f32),
        ],
        compiler_params=pltpu.CompilerParams(vmem_limit_bytes=VMEM_LIMIT),
        cost_estimate=pl.CostEstimate(
            flops=6 * seq_len * width * columns, bytes_accessed=18 * 2**20, transcendentals=0
        ),
        name="weight_products",
    )(firsts, *pieces, cols, *weights, grad_q, grad_kv)


def reduce_along(chunks, axis, own):
    size = chunks.shape[0]
    total = pick(chunks, own).astype(f32)
    for step in range(1, size):
        total += ring(pick(chunks, (own + step) % size), axis, step).astype(f32)
    return total


def per_device(
    hidden_in, grad_out, saved_qkv, saved_attn, w_qkv, w_out, mod_table, timestep, text_count
):
    c, yl, x = (lax.axis_index(name) for name in ("c", "yl", "x"))
    yh, z = lax.axis_index("yh"), lax.axis_index("z")
    chip_y = yh * 2 + yl
    shard_rows, width = hidden_in.shape[1:]
    seq_len = saved_qkv.shape[1]
    text_len = seq_len // 4
    first_row = (c * 4 + x) * shard_rows

    grad_own = rehome(grad_out[0])
    numbers = rehome(jnp.concatenate([timestep, text_count]))
    wouts = (w_out, move_weight(w_out))
    w_qkv = w_qkv.transpose(1, 0, 2)
    weights = (w_qkv, move_weight(w_qkv))
    grad_pieces, firsts = gather_pieces(grad_own, x, c)
    hidden_own = rehome(after(hidden_in[0], grad_own))
    attn = rehome(after(saved_attn[0], *grad_pieces[1:3]))
    qkv = rehome(after(saved_qkv[0].transpose(1, 0, 2), *grad_pieces[3:5]))

    hidden_f = hidden_own.astype(f32)
    centered = hidden_f - jnp.mean(hidden_f, axis=1, keepdims=True)
    inv_std = lax.rsqrt(jnp.mean(centered * centered, axis=1, keepdims=True) + norm_eps)
    normed = centered * inv_std
    normed_pieces, _ = gather_pieces(normed.astype(bf16), x, c, *grad_pieces[3:5])

    modulation = mod_table[numbers[0]].astype(f32)
    rows = jnp.stack(
        [modulation[0, 0], 1.0 + modulation[0, 1], modulation[0, 2]]
        + [modulation[1, 0], 1.0 + modulation[1, 1], modulation[1, 2]]
        + [jnp.zeros((width,), f32)] * 2
    )
    cols = rows.T
    gates = jnp.concatenate([rows[2:3], rows[5:6], jnp.zeros((6, width), f32)])

    attn_grad, out_term, gate_sums = grad_products(
        grad_pieces, firsts, gates, cols, wouts, attn, text_len
    )
    attn_grad = after(attn_grad, *normed_pieces[1:3])
    grad_q, grad_kv = attention_grads(qkv, attn_grad, numbers[1:], text_len)
    grad_q = after(grad_q, *normed_pieces[3:5])
    out_y = reduce_along(after(out_term, grad_q).reshape(4, 8, 1, 96, 256), Y, chip_y)

    keep = stays().astype(jnp.int32)
    away = mixed_half(jnp.stack([keep, 1 - c]), grad_q, grad_kv, weights)
    got = swap_core(away).reshape(4, shard_rows, width)
    term, sums = weight_products(
        normed_pieces, firsts, cols, weights, grad_q, grad_kv, text_len
    )
    kept = mixed_half(jnp.stack([keep, c]), grad_q, grad_kv, weights).reshape(4, shard_rows, width)

    def both(place):
        return pick(kept, place).astype(f32) + pick(got, place).astype(f32)

    near = [ring(both((x + step) % 4).astype(bf16), "x", step) for step in (1, 3)]
    far = ring(after(both((x + 2) % 4).astype(bf16), *near), "x", 2)
    mixed_grad = both(x) + near[0].astype(f32) + near[1].astype(f32) + far.astype(f32)

    term_y = reduce_along(term.reshape(4, 8, 3, 96, 256), Y, chip_y)

    mod_grad = jnp.stack([sums[0], sums[2], gate_sums[0], sums[1], sums[3], gate_sums[1]])
    pieces = mod_grad.reshape(6, 2, 4, width // 8).transpose(1, 2, 0, 3)
    pieces = pick(pieces, c) + swap_core(pick(pieces, 1 - c))
    own_mod = reduce_along(pieces, "x", x).reshape(9, 256)
    own_mod = jnp.concatenate([own_mod, jnp.zeros((7, 256), f32)]).astype(bf16)
    chunk = jnp.arange(32, dtype=jnp.int32).reshape(2, 8, 2).transpose(0, 2, 1).reshape(4, 8)
    table_term = jnp.where((chunk == numbers[0])[:, :, None, None], own_mod, 0.0).astype(bf16)
    table_y = reduce_along(after(table_term, *near), Y, chip_y)

    chunks = [term_y.reshape(8, 288, 256), out_y.reshape(8, 96, 256), table_y]
    whole = rehome(reduce_along(jnp.concatenate(chunks, axis=1).astype(bf16), "z", z).astype(bf16))
    whole = whole.astype(f32)
    grad_w_qkv = whole[:288].reshape(3, 96, 256).transpose(1, 0, 2)
    grad_w_out = whole[288:384]
    grad_table = whole[384:393].reshape(1, 2, 3, width // 8)

    scale_own = jnp.where(first_row >= text_len, rows[4], rows[1])[None]
    scaled = mixed_grad * scale_own
    branch = inv_std * (
        scaled
        - jnp.mean(scaled, axis=1, keepdims=True)
        - normed * jnp.mean(scaled * normed, axis=1, keepdims=True)
    )
    grad_in = rehome(branch.astype(bf16))[None]
    return (grad_in, grad_w_qkv, grad_w_out, grad_table)


def solution(mesh):
    fine = Mesh(mesh.devices.reshape(tuple(AXES.values())), tuple(AXES))
    dp, tensor = ("yh", "z", "c"), ("yl", "x")
    in_specs = (
        P(dp, tensor, None),
        P(dp, tensor, None),
        P(dp, None, None, tensor),
        P(dp, None, tensor),
        P(None, None, tensor),
        P(None, tensor),
        P(),
        P(dp),
        P(dp),
    )
    out_specs = (
        P(dp, tensor, None),
        P(dp, None, tensor),
        P(dp, tensor),
        P(dp, None, None, tensor),
    )
    return jax.shard_map(
        per_device, mesh=fine, in_specs=in_specs, out_specs=out_specs, check_vma=False
    )
```
